32 devices in a mesh: groups: 2 (over x), shard: 16 (over z, y, core).
Axes of the slice: x: 2, y: 2, z: 4, core: 2. Of those that a mesh axis runs over, the one named last changes fastest.
Arguments:
- kv_store: bfloat16 [64, 256, 2048], P(('groups', 'shard')), parts along dimension 0, may hold values from -6 to 6
- block_order: int32 [64], P(('groups', 'shard')), parts along dimension 0, may hold values from 0 to 31, as said below
- lengths: int32 [16], P('groups'), parts along dimension 0, may hold values from 1 to 12, as said below
- row_positions: int32 [16, 128], P('groups'), parts along dimension 0, may hold values from 0 to 3071, as said below
- queries: bfloat16 [256, 65536], P('groups', 'shard'), parts along dimension 0, may hold values from -48 to 48
- fresh_rows: bfloat16 [256, 16384], P('groups', 'shard'), parts along dimension 0, may hold values from -280 to 280
Outputs:
- attended: bfloat16 [256, 65536], P('groups', 'shard'), parts along dimension 0
The draws below stay inside these ranges and needn't reach their ends.
There are 2 independent parts, one for each index of `groups`. The reference program is written for one: setup_inputs(seed, part) draws one part's arguments, and reference() takes and returns one part's arrays. A program takes and returns all parts, laid end to end along the dimension named above; each array names one. Nothing has to cross between parts.
Inputs may be any that keep to these rules, and one draw needn't show every extreme that they name: Each request has at least one block, the lengths sum to 32, and the longest request has exactly 12 blocks. Request r and request r + 4 together have at most 16 blocks, exactly so for the pair of the longest request. `row_positions`: each request's positions are non-decreasing and lie below 256 times its length; its last recomputed row is its last token, 256 lengths[r] - 1. `block_order`: A permutation; the 2 slots of one device (slots 2 d to 2 d + 1) hold blocks of requests r1, r2 with r1 % (4) != r2 % 4.
All inputs are finite; a program needn't handle non-finite values.
Results may differ from the reference program's by a relative error of at most 0.0041.
Values may be sent and summed in bfloat16 or wider, within the bound.
A program may use at most 64 MiB of HBM per device.

```python
import math
import jax
import jax.numpy as jnp
from jax import lax

QH = 64
KVH = 8
HD = 128
BLOCK = 256
REQS = 8
ROWS_REQ = 128
NB = 32
MOST = 12


def query_base(base_key):
    normal_key = jax.random.fold_in(base_key, 501)
    drawn = jnp.clip(jax.random.normal(normal_key, (ROWS_REQ, REQS, KVH, QH // KVH, HD), jnp.float32), -6.0, 6.0)
    return drawn


def length_table(base_key):
    table_key = jax.random.fold_in(base_key, 701)
    longest_key = jax.random.fold_in(table_key, 1)
    split_key = jax.random.fold_in(table_key, 2)
    flip_key = jax.random.fold_in(table_key, 3)
    half_reqs = REQS // 2
    others = half_reqs - 1
    longest = jax.random.randint(longest_key, (), 0, REQS)
    long_pair = longest % half_reqs
    rest = NB - NB // 2
    pair_ids = jnp.arange(half_reqs, dtype=jnp.int32)
    rank = pair_ids - (pair_ids > long_pair).astype(jnp.int32)
    totals = rest // others + (rank < rest % others).astype(jnp.int32)
    first = jax.random.randint(split_key, (half_reqs,), 1, totals)
    flips = jax.random.randint(flip_key, (half_reqs,), 0, 2)
    low_len = jnp.where(flips == 1, first, totals - first)
    high_len = totals - low_len
    partner_len = NB // 2 - MOST
    long_low = jnp.where(longest < half_reqs, MOST, partner_len)
    long_high = jnp.where(longest < half_reqs, partner_len, MOST)
    low_len = jnp.where(pair_ids == long_pair, long_low, low_len)
    high_len = jnp.where(pair_ids == long_pair, long_high, high_len)
    return jnp.concatenate([low_len, high_len]).astype(jnp.int32)


def draw_lengths(key, part):
    return length_table(key)


def draw_block_order(key, part):
    table = length_table(key)
    starts = jnp.cumsum(table) - table
    block_ids = jnp.arange(NB, dtype=jnp.int32)
    req_of = jnp.sum((block_ids[:, None] >= starts[None, 1:]).astype(jnp.int32), axis=1)
    pair_of = req_of % (REQS // 2)
    ranks = jax.random.permutation(jax.random.fold_in(key, 801), NB).astype(jnp.int32)
    sorted_ids = jnp.argsort(pair_of * NB + ranks, stable=True).astype(jnp.int32)
    holders = NB // 2
    device_perm = jax.random.permutation(jax.random.fold_in(key, 802), holders).astype(jnp.int32)
    swapped = jax.random.randint(jax.random.fold_in(key, 803), (holders,), 0, 2)
    slot_pick = jnp.arange(2, dtype=jnp.int32)
    flipped = jnp.abs(slot_pick[None, :] - swapped[:, None])
    places = device_perm[:, None] + holders * flipped
    return sorted_ids[places.reshape(NB)].astype(jnp.int32)


def draw_row_positions(key, part):
    table = length_table(key)
    pick_key = jax.random.fold_in(key, 702)
    last_row = BLOCK * table - 1
    picks = jax.random.randint(pick_key, (REQS, ROWS_REQ - 1), 0, last_row[:, None])
    picks = jnp.sort(picks, axis=1)
    return jnp.concatenate([picks, last_row[:, None]], axis=1).astype(jnp.int32)


def draw_queries(key, part):
    return query_base(key).reshape(ROWS_REQ, REQS * QH * HD).astype(jnp.bfloat16)


def draw_fresh_rows(key, part):
    drawn = query_base(key)
    noise_key = jax.random.fold_in(key, 503)
    value_key = jax.random.fold_in(key, 504)
    noise = jnp.clip(jax.random.normal(noise_key, (ROWS_REQ, REQS, KVH, HD), jnp.float32), -6.0, 6.0)
    fresh_keys = 0.7 * jnp.sum(drawn, axis=3) + 0.5 * noise
    fresh_values = jnp.clip(jax.random.normal(value_key, (ROWS_REQ, REQS, KVH, HD), jnp.float32), -6.0, 6.0)
    stacked = jnp.stack([fresh_keys, fresh_values], axis=3)
    return stacked.reshape(ROWS_REQ, REQS * KVH * 2 * HD).astype(jnp.bfloat16)


def level_of(rng, shape, split, least, largest):
    factor_of, own = 1.0, jax.random.fold_in(rng, 6)
    for position, shards_of in split:
        heights = jnp.exp(jax.random.uniform(jax.random.fold_in(own, position), (shards_of,), jnp.float32, least / len(split), largest / len(split)))
        factor_of = factor_of * jnp.repeat(heights, shape[position] // shards_of).reshape([-1 if axis == position else 1 for axis in range(len(shape))])
    return factor_of


def scatter_about(stream_key, shape, width, reach, shards=(), kind=jnp.bfloat16):
    entries = jax.random.normal(stream_key, shape, jnp.float32) * width
    if len(shards) > 0:
        entries = level_of(stream_key, shape, shards, -0.22, 0.18) * entries
    return jnp.clip(entries, min=-reach, max=reach).astype(kind)


def setup_inputs(seed: int = 0, part: int = 0) -> dict:
    key_of = jax.random.split(jax.random.key(seed), 7)
    part_splits = jax.random.split(jax.random.fold_in(key_of[6], part), 7)
    kv_store = scatter_about(part_splits[0], (NB, BLOCK, 2 * KVH * HD), 1.0, 6.0, ((0, 16),))
    block_order = draw_block_order(jax.random.fold_in(jax.random.fold_in(key_of[6], part), 71), part)
    lengths = draw_lengths(jax.random.fold_in(jax.random.fold_in(key_of[6], part), 71), part)
    row_positions = draw_row_positions(jax.random.fold_in(jax.random.fold_in(key_of[6], part), 71), part)
    queries = draw_queries(jax.random.fold_in(jax.random.fold_in(key_of[6], part), 71), part)
    fresh_rows = draw_fresh_rows(jax.random.fold_in(jax.random.fold_in(key_of[6], part), 71), part)
    return {"kv_store": kv_store, "block_order": block_order, "lengths": lengths, "row_positions": row_positions, "queries": queries, "fresh_rows": fresh_rows}


ROPE_BASE = 500000.0
NEG_FILL = -1e+30

def frequencies(half_size):
    step_ids = jnp.arange(half_size, dtype=jnp.float32)
    return jnp.exp(-math.log(ROPE_BASE) * step_ids / half_size)

def rotate(vectors, turn_angle):
    half_size = vectors.shape[-1] // 2
    cosine = jnp.cos(turn_angle)
    sine_part = jnp.sin(turn_angle)
    lower_half = vectors[..., :half_size]
    upper_half = vectors[..., half_size:]
    return jnp.concatenate([lower_half * cosine - upper_half * sine_part, upper_half * cosine + lower_half * sine_part], axis=-1)

def round_trip(values):
    return lax.optimization_barrier(values.astype(jnp.bfloat16)).astype(jnp.float32)

def merge_state(acc_state, block_term):
    old_top, old_sum, old_out = acc_state
    new_top, new_sum, new_out = block_term
    joined_top = jnp.maximum(old_top, new_top)
    old_factor = jnp.exp(old_top - joined_top)
    new_factor = jnp.exp(new_top - joined_top)
    return (joined_top, old_sum * old_factor + new_sum * new_factor, old_out * old_factor[..., None] + new_out * new_factor[..., None])

def reference_partial(query_set, row_limit, key_block, value_block, offset, score_scale):
    scores = jnp.einsum('ncgd,tcd->cgnt', query_set, key_block) * score_scale
    key_positions = offset + jnp.arange(key_block.shape[0], dtype=jnp.int32)
    allowed = key_positions[None, :] < row_limit[:, None]
    block_top = lax.optimization_barrier(jnp.max(jnp.where(allowed, scores, NEG_FILL), axis=-1))
    weights = round_trip(jnp.where(allowed, jnp.exp(scores - block_top[..., None]), 0.0))
    weight_sum = lax.optimization_barrier(jnp.sum(weights, axis=-1))
    summed = jnp.einsum('cgnt,tcd->cgnd', weights, value_block)
    return (block_top, weight_sum, summed)

def reference(kv_store, block_order, lengths, row_positions, queries, fresh_rows):
    group_size = QH // KVH
    score_scale = 1.0 / math.sqrt(HD)
    frequency = frequencies(HD // 2)
    lengths = lengths.astype(jnp.int32)
    starts = (jnp.cumsum(lengths) - lengths).astype(jnp.int32)
    block_ids = jnp.arange(NB, dtype=jnp.int32)
    inverse = jnp.zeros((NB,), jnp.int32).at[block_order.astype(jnp.int32)].set(block_ids)
    req_of = lax.optimization_barrier(jnp.sum((block_ids[:, None] >= starts[None, 1:]).astype(jnp.int32), axis=1)).astype(jnp.int32)
    pos_of = (block_ids - starts[req_of]).astype(jnp.int32)
    row_limits = row_positions.astype(jnp.int32)
    row_angle = jnp.transpose(row_limits).astype(jnp.float32)[..., None] * frequency
    query_f32 = queries.reshape(ROWS_REQ, REQS, KVH, group_size, HD).astype(jnp.float32)
    rotated_q = round_trip(rotate(query_f32, row_angle[:, :, None, None, :]))
    fresh_split = fresh_rows.reshape(ROWS_REQ, REQS, KVH, 2, HD)
    own_key = round_trip(rotate(fresh_split[:, :, :, 0].astype(jnp.float32), row_angle[:, :, None, :]))
    own_value = fresh_split[:, :, :, 1].astype(jnp.float32)
    own_score = jnp.einsum('nrcgd,nrcd->rcgn', rotated_q, own_key) * score_scale
    own_out = jnp.broadcast_to(jnp.transpose(own_value, (1, 2, 0, 3))[:, :, None], (REQS, KVH, group_size, ROWS_REQ, HD))
    start_state = (own_score, jnp.ones_like(own_score), own_out)
    query_by_req = jnp.transpose(rotated_q, (1, 0, 2, 3, 4))

    def one_block(carried, block_id):
        slot_id = inverse[block_id]
        request = req_of[block_id]
        offset = pos_of[block_id] * BLOCK
        block_kv = lax.dynamic_index_in_dim(kv_store, slot_id, 0, keepdims=False).reshape(BLOCK, KVH, 2, HD)
        key_block = round_trip(rotate(block_kv[:, :, 0].astype(jnp.float32), offset.astype(jnp.float32) * frequency))
        query_set = lax.dynamic_index_in_dim(query_by_req, request, 0, keepdims=False)
        row_limit = lax.dynamic_index_in_dim(row_limits, request, 0, keepdims=False)
        block_term = reference_partial(query_set, row_limit, key_block, block_kv[:, :, 1].astype(jnp.float32), offset, score_scale)
        older = tuple((lax.dynamic_index_in_dim(member, request, 0, keepdims=False) for member in carried))
        joined = merge_state(older, block_term)
        carried = tuple((lax.dynamic_update_index_in_dim(whole, piece, request, 0) for whole, piece in zip(carried, joined)))
        return (carried, None)
    final_state, unused = lax.scan(one_block, start_state, block_ids)
    normalized = final_state[2] / final_state[1][..., None]
    return jnp.transpose(normalized, (3, 0, 1, 2, 4)).reshape(ROWS_REQ, REQS * QH * HD).astype(jnp.bfloat16)
```

```python
import functools
import math

import jax
import jax.numpy as jnp
from jax import lax
from jax.experimental import pallas as pl
from jax.experimental.pallas import tpu as pltpu
from jax.sharding import PartitionSpec as P

QH = 64
KVH = 8
HD = 128
REQS = 8
GROUP = QH // KVH
PAIRS = REQS // 2

ROPE_BASE = 500000.0
NEG_FILL = -1e30
NEG_START = -1e29
LOG2E = 1.4426950408889634
NT = (((1,), (1,)), ((), ()))
TN = (((0,), (0,)), ((), ()))


def frequencies(half_size):
    step_ids = jnp.arange(half_size, dtype=jnp.float32)
    return jnp.exp(-math.log(ROPE_BASE) * step_ids / half_size)


def turn_tables(positions):
    angle = positions.astype(jnp.float32)[..., None] * frequencies(HD // 2)
    cosine, sine = jnp.cos(angle), jnp.sin(angle)
    return (
        jnp.concatenate([cosine, cosine], axis=-1),
        jnp.concatenate([-sine, sine], axis=-1),
    )


def turned(x, cosine, sine):
    x = x.astype(jnp.float32)
    return (x * cosine + pltpu.roll(x, HD // 2, 1) * sine).astype(jnp.bfloat16)


def lookup(values, table_ids, where_at):
    return jnp.sum(jnp.where(where_at[..., None] == table_ids, values, 0), axis=-1)


def pack_kernel(heads, sel_ref, kv_ref, cos_ref, sin_ref, out_ref):
    for c in range(heads):
        key, value = pl.ds(2 * c * HD, HD), pl.ds((2 * c + 1) * HD, HD)
        out_ref[0, :, key] = turned(kv_ref[0, :, key], cos_ref[0], sin_ref[0])
        out_ref[0, :, value] = kv_ref[0, :, value]


def pack(sel, kv_store, cosine, sine, per_req, chunks, chunk):
    block_len, width = kv_store.shape[1:]
    part = width // (per_req * chunks)
    peers = PAIRS * per_req
    grid_spec = pltpu.PrefetchScalarGridSpec(
        num_scalar_prefetch=1,
        grid=(peers,),
        in_specs=[
            pl.BlockSpec(
                (1, block_len, part),
                lambda i, sel: (sel[i // per_req], 0, (i % per_req) * chunks + chunk),
            ),
            pl.BlockSpec((1, 1, HD), lambda i, sel: (sel[i // per_req], 0, 0)),
            pl.BlockSpec((1, 1, HD), lambda i, sel: (sel[i // per_req], 0, 0)),
        ],
        out_specs=pl.BlockSpec((1, block_len, part), lambda i, sel: (i, 0, 0)),
    )
    return pl.pallas_call(
        functools.partial(pack_kernel, part // (2 * HD)),
        grid_spec=grid_spec,
        out_shape=jax.ShapeDtypeStruct((peers, block_len, part), kv_store.dtype),
        compiler_params=pltpu.CompilerParams(vmem_limit_bytes=16 << 20),
        cost_estimate=pl.CostEstimate(
            flops=3 * peers * block_len * part, bytes_accessed=4 * peers * block_len * part, transcendentals=0
        ),
        name="pack",
    )(sel, kv_store, cosine, sine)


def attend_kernel(
    scale,
    side_ref,
    base_ref,
    kv_ref,
    q0_ref,
    q1_ref,
    fresh_ref,
    cos_ref,
    sin_ref,
    limit_ref,
    o0_ref,
    lse0_ref,
    o1_ref,
    lse1_ref,
    qs,
    top,
    total,
    acc,
):
    j = pl.program_id(1)
    rows = q0_ref.shape[0]
    lanes = rows * GROUP

    @pl.when(j == 0)
    def _():
        for side, q_ref in enumerate((q0_ref, q1_ref)):
            for g in range(GROUP):
                qs[side, pl.ds(g * rows, rows), :] = turned(q_ref[:, pl.ds(g * HD, HD)], cos_ref[side], sin_ref[side])
        own_key = turned(fresh_ref[:, pl.ds(0, HD)], cos_ref[0], sin_ref[0])
        own = lax.dot_general(own_key, qs[0], NT, preferred_element_type=jnp.float32)
        row_of = lax.broadcasted_iota(jnp.int32, (rows, lanes), 0)
        lane_of = lax.broadcasted_iota(jnp.int32, (rows, lanes), 1) % rows
        top[0] = jnp.sum(jnp.where(row_of == lane_of, own, 0.0), axis=0, keepdims=True)
        total[0] = jnp.ones((1, lanes), jnp.float32)
        own_value = fresh_ref[:, pl.ds(HD, HD)].astype(jnp.float32).T
        for g in range(GROUP):
            acc[0, :, pl.ds(g * rows, rows)] = own_value
        top[1] = jnp.full((1, lanes), NEG_START, jnp.float32)
        total[1] = jnp.zeros((1, lanes), jnp.float32)
        acc[1] = jnp.zeros((HD, lanes), jnp.float32)

    side = side_ref[j]

    @pl.when(side >= 0)
    def _():
        keys = kv_ref[0, :, pl.ds(0, HD)]
        values = kv_ref[0, :, pl.ds(HD, HD)]
        scores = lax.dot_general(keys, qs[side], NT, preferred_element_type=jnp.float32)
        token = base_ref[j] + lax.broadcasted_iota(jnp.int32, scores.shape, 0)
        scores = jnp.where(token < limit_ref[side], scores, NEG_FILL)
        old_top = top[side]
        new_top = jnp.maximum(old_top, jnp.max(scores, axis=0, keepdims=True))
        factor = jnp.exp2((old_top - new_top) * (scale * LOG2E))
        weights = jnp.exp2((scores - new_top) * (scale * LOG2E)).astype(jnp.bfloat16)
        top[side] = new_top
        total[side] = total[side] * factor + jnp.sum(weights.astype(jnp.float32), axis=0, keepdims=True)
        acc[side] = acc[side] * factor + lax.dot_general(values, weights, TN, preferred_element_type=jnp.float32)

    @pl.when(j == pl.num_programs(1) - 1)
    def _():
        o0_ref[0] = acc[0] * (1.0 / total[0])
        lse0_ref[0] = top[0] * scale + jnp.log(total[0])
        some = total[1] > 0.0
        safe = jnp.where(some, total[1], 1.0)
        o1_ref[0] = (acc[1] * (1.0 / safe)).astype(jnp.bfloat16)
        lse1_ref[0] = jnp.where(some, top[1] * scale + jnp.log(safe), NEG_FILL)


def attend(side, base, received, queries, partner_queries, fresh, cosine, sine, limits, heads, first):
    peers, block_len = received.shape[:2]
    rows = queries.shape[0]
    lanes = rows * GROUP
    grid_spec = pltpu.PrefetchScalarGridSpec(
        num_scalar_prefetch=2,
        grid=(heads, peers),
        in_specs=[
            pl.BlockSpec((1, block_len, 2 * HD), lambda c, j, s, b: (j, 0, c)),
            pl.BlockSpec((rows, GROUP * HD), lambda c, j, s, b: (0, first + c)),
            pl.BlockSpec((rows, GROUP * HD), lambda c, j, s, b: (0, c)),
            pl.BlockSpec((rows, 2 * HD), lambda c, j, s, b: (0, first + c)),
            pl.BlockSpec((2, rows, HD), lambda c, j, s, b: (0, 0, 0)),
            pl.BlockSpec((2, rows, HD), lambda c, j, s, b: (0, 0, 0)),
            pl.BlockSpec((2, 1, lanes), lambda c, j, s, b: (0, 0, 0)),
        ],
        out_specs=[
            pl.BlockSpec((1, HD, lanes), lambda c, j, s, b: (c, 0, 0)),
            pl.BlockSpec((1, 1, lanes), lambda c, j, s, b: (c, 0, 0)),
            pl.BlockSpec((1, HD, lanes), lambda c, j, s, b: (c, 0, 0)),
            pl.BlockSpec((1, 1, lanes), lambda c, j, s, b: (c, 0, 0)),
        ],
        scratch_shapes=[
            pltpu.VMEM((2, lanes, HD), jnp.bfloat16),
            pltpu.VMEM((2, 1, lanes), jnp.float32),
            pltpu.VMEM((2, 1, lanes), jnp.float32),
            pltpu.VMEM((2, HD, lanes), jnp.float32),
        ],
    )
    return pl.pallas_call(
        functools.partial(attend_kernel, 1.0 / math.sqrt(HD)),
        grid_spec=grid_spec,
        out_shape=[
            jax.ShapeDtypeStruct((heads, HD, lanes), jnp.float32),
            jax.ShapeDtypeStruct((heads, 1, lanes), jnp.float32),
            jax.ShapeDtypeStruct((heads, HD, lanes), jnp.bfloat16),
            jax.ShapeDtypeStruct((heads, 1, lanes), jnp.float32),
        ],
        compiler_params=pltpu.CompilerParams(vmem_limit_bytes=32 << 20),
        cost_estimate=pl.CostEstimate(
            flops=4 * heads * peers * block_len * lanes * HD,
            bytes_accessed=2 * heads * peers * block_len * 2 * HD,
            transcendentals=heads * peers * block_len * lanes,
        ),
        name="attend",
    )(side, base, received, queries, partner_queries, fresh, cosine, sine, limits)


def merge_kernel(o0_ref, lse0_ref, o1_ref, lse1_ref, out_ref):
    rows = out_ref.shape[0]
    larger = jnp.maximum(lse0_ref[0], lse1_ref[0])
    first, second = jnp.exp(lse0_ref[0] - larger), jnp.exp(lse1_ref[0] - larger)
    scaled = 1.0 / (first + second)
    joined = o0_ref[0] * (first * scaled) + o1_ref[0].astype(jnp.float32) * (second * scaled)
    for g in range(GROUP):
        out_ref[:, pl.ds(g * HD, HD)] = joined[:, g * rows : (g + 1) * rows].T.astype(out_ref.dtype)


def merge(o0, lse0, o1, lse1, rows):
    heads, _, lanes = o0.shape
    wide = pl.BlockSpec((1, HD, lanes), lambda c: (c, 0, 0))
    thin = pl.BlockSpec((1, 1, lanes), lambda c: (c, 0, 0))
    return pl.pallas_call(
        merge_kernel,
        grid=(heads,),
        in_specs=[wide, thin, wide, thin],
        out_specs=pl.BlockSpec((rows, GROUP * HD), lambda c: (0, c)),
        out_shape=jax.ShapeDtypeStruct((rows, heads * GROUP * HD), jnp.bfloat16),
        compiler_params=pltpu.CompilerParams(vmem_limit_bytes=32 << 20),
        name="merge",
    )(o0, lse0, o1, lse1)


def bookkeeping(n_shard, block_order, lengths, block_len):
    blk_dev = block_order.shape[0]
    half = n_shard // 2
    per_req = n_shard // REQS
    me = lax.axis_index("shard")
    my_half, my_req = me // half, me // per_req
    req_ids = jnp.arange(REQS, dtype=jnp.int32)
    starts = jnp.sum(jnp.where(req_ids[None, :] < req_ids[:, None], lengths[None, :], 0), axis=1)

    def place(blocks):
        req = jnp.sum((blocks[..., None] >= starts[1:]).astype(jnp.int32), axis=-1)
        return req, (blocks - lookup(starts, req_ids, req)) * block_len

    dest, offset = place(block_order)
    pair_ids = jnp.arange(PAIRS, dtype=jnp.int32)
    slot_ids = jnp.arange(blk_dev, dtype=jnp.int32)
    sel = jnp.sum(jnp.where((dest % PAIRS)[None, :] == pair_ids[:, None], slot_ids[None, :], 0), axis=1)
    all_order = lax.all_gather(block_order, "shard", axis=0, tiled=True).reshape(2, half, blk_dev)
    near = jnp.where(my_half == 0, all_order[0], all_order[1])
    near_req, near_offset = place(near)
    mine = near_req % PAIRS == my_req % PAIRS
    side = jnp.sum(jnp.where(mine, jnp.where(near_req == my_req, 1, 2), 0), axis=1) - 1
    base = jnp.sum(jnp.where(mine, near_offset, 0), axis=1)
    return sel, offset, side, base, my_req


def shards(kv_store, block_order, lengths, row_positions, queries, fresh_rows):
    n_shard = lax.axis_size("shard")
    half = n_shard // 2
    per_req = n_shard // REQS
    block_len, width = kv_store.shape[1:]
    heads = width // (per_req * 2 * HD)
    chunks = heads if heads <= 4 else 4
    per_chunk = heads // chunks
    rows = queries.shape[0]
    swap = [(i, (i + half) % n_shard) for i in range(n_shard)]
    halves = [list(range(half)), list(range(half, n_shard))]
    sel, offset, side, base, my_req = bookkeeping(n_shard, block_order, lengths, block_len)
    block_cos, block_sin = turn_tables(offset[:, None])
    both = jnp.stack(
        [
            lax.dynamic_index_in_dim(row_positions, my_req, 0, keepdims=False),
            lax.dynamic_index_in_dim(row_positions, (my_req + PAIRS) % REQS, 0, keepdims=False),
        ]
    )
    row_cos, row_sin = turn_tables(both)
    limits = jnp.tile(both, (1, GROUP))[:, None, :]
    q_width = per_chunk * GROUP * HD
    done = []
    for chunk in range(chunks):
        sent = pack(sel, kv_store, block_cos, block_sin, per_req, chunks, chunk)
        received = lax.all_to_all(
            sent, "shard", split_axis=0, concat_axis=0, axis_index_groups=halves, tiled=True
        )
        partner_q = lax.ppermute(queries[:, chunk * q_width : (chunk + 1) * q_width], "shard", swap)
        o0, lse0, o1, lse1 = attend(
            side, base, received, queries, partner_q, fresh_rows, row_cos, row_sin, limits, per_chunk, chunk * per_chunk
        )
        o1 = lax.ppermute(o1, "shard", swap)
        lse1 = lax.ppermute(lse1, "shard", swap)
        done.append(merge(o0, lse0, o1, lse1, rows))
    return jnp.concatenate(done, axis=1)


def solution(mesh):
    in_specs = (
        P(("groups", "shard"), None, None),
        P(("groups", "shard")),
        P("groups"),
        P("groups", None),
        P("groups", "shard"),
        P("groups", "shard"),
    )
    out_specs = P("groups", "shard")
    return jax.shard_map(shards, mesh=mesh, in_specs=in_specs, out_specs=out_specs, check_vma=False)
```

```python
import functools
import math

import jax
import jax.numpy as jnp
from jax import lax
from jax.experimental import pallas as pl
from jax.experimental.pallas import tpu as pltpu
from jax.sharding import PartitionSpec as P

QH = 64
KVH = 8
HD = 128
REQS = 8
GROUP = QH // KVH
PAIRS = REQS // 2

ROPE_BASE = 500000.0
NEG_FILL = -1e30
NEG_START = -1e29
LOG2E = 1.4426950408889634
NT = (((1,), (1,)), ((), ()))
TN = (((0,), (0,)), ((), ()))


def frequencies(half_size):
    step_ids = jnp.arange(half_size, dtype=jnp.float32)
    return jnp.exp(-math.log(ROPE_BASE) * step_ids / half_size)


def turn_tables(positions):
    angle = positions.astype(jnp.float32)[..., None] * frequencies(HD // 2)
    cosine, sine = jnp.cos(angle), jnp.sin(angle)
    return (
        jnp.concatenate([cosine, cosine], axis=-1),
        jnp.concatenate([-sine, sine], axis=-1),
    )


def turned(x, cosine, sine):
    x = x.astype(jnp.float32)
    return (x * cosine + pltpu.roll(x, HD // 2, 1) * sine).astype(jnp.bfloat16)


def lookup(values, table_ids, where_at):
    return jnp.sum(jnp.where(where_at[..., None] == table_ids, values, 0), axis=-1)


def whole_kernel(
    n,
    scale,
    sel_ref,
    kv_ref,
    bcos_ref,
    bsin_ref,
    meta_ref,
    q_ref,
    fresh_ref,
    cos_ref,
    sin_ref,
    limit_ref,
    req_ref,
    out_ref,
    sent,
    received,
    metas,
    partner_q,
    qs,
    top,
    total,
    acc,
    o0,
    lse0,
    o1,
    lse1,
    o1_in,
    lse1_in,
    kv_send,
    kv_recv,
    meta_send,
    meta_recv,
    q_send,
    q_recv,
    o_send,
    o_recv,
    l_send,
    l_recv,
    local_sem,
):
    heads, peers, block_len, _ = sent.shape
    rows = q_ref.shape[0]
    lanes = rows * GROUP
    q_width = GROUP * HD
    per_req = n // REQS
    device = lax.axis_index("shard")
    me = lax.rem(device, peers)
    first_peer = device - me
    partner = lax.rem(device + peers, n)
    log_scale = scale * LOG2E

    def remote(src, dst, send, recv, target):
        return pltpu.make_async_remote_copy(
            src_ref=src,
            dst_ref=dst,
            send_sem=send,
            recv_sem=recv,
            device_id={"shard": target},
            device_id_type=pl.DeviceIdType.MESH,
        )

    def kv_copy(c, i, slot):
        return remote(sent.at[c, i], received.at[c, slot], kv_send.at[c, i], kv_recv.at[c, slot], first_peer + i)

    def meta_copy(i, slot):
        return remote(
            meta_ref.at[i // per_req], metas.at[slot], meta_send.at[i], meta_recv.at[slot], first_peer + i
        )

    def q_copy(c):
        columns = pl.ds(pl.multiple_of(c * q_width, q_width), q_width)
        return remote(q_ref.at[:, columns], partner_q.at[c], q_send.at[c], q_recv.at[c], partner)

    def o_copy(c):
        return remote(o1.at[c], o1_in.at[c], o_send.at[c], o_recv.at[c], partner)

    def l_copy(c):
        return remote(lse1.at[c], lse1_in.at[c], l_send.at[c], l_recv.at[c], partner)

    def own_kv(c):
        return pltpu.make_async_copy(sent.at[c, me], received.at[c, me], local_sem.at[c])

    barrier = pltpu.get_barrier_semaphore()
    pl.semaphore_signal(barrier, inc=1, device_id={"shard": partner}, device_id_type=pl.DeviceIdType.MESH)

    def greet(t, carry):
        pl.semaphore_signal(
            barrier,
            inc=1,
            device_id={"shard": first_peer + lax.rem(me + t, peers)},
            device_id_type=pl.DeviceIdType.MESH,
        )
        return carry

    lax.fori_loop(1, peers, greet, 0)
    pl.semaphore_wait(barrier, peers)

    own_meta = pltpu.make_async_copy(meta_ref.at[me // per_req], metas.at[me], local_sem.at[heads])
    own_meta.start()

    def tell(t, carry):
        meta_copy(lax.rem(me + t, peers), me).start()
        return carry

    lax.fori_loop(1, peers, tell, 0)

    def pack_chunk(c, carry):
        q_copy(c).start()

        def pack(t, carry):
            i = lax.rem(me + t, peers)
            pair, group = i // per_req, lax.rem(i, per_req)
            sel = sel_ref[pair]
            column = pl.multiple_of((group * heads + c) * 2 * HD, 2 * HD)
            key = kv_ref[sel, :, pl.ds(column, HD)]
            sent[c, i, :, pl.ds(0, HD)] = turned(key, bcos_ref[sel], bsin_ref[sel])
            sent[c, i, :, pl.ds(HD, HD)] = kv_ref[sel, :, pl.ds(pl.multiple_of(column + HD, HD), HD)]

            @pl.when(t > 0)
            def _():
                kv_copy(c, i, me).start()

            @pl.when(t == 0)
            def _():
                own_kv(c).start()

            return carry

        return lax.fori_loop(0, peers, pack, carry)

    lax.fori_loop(0, heads, pack_chunk, 0)

    def hear(t, carry):
        j = lax.rem(me + t, peers)
        meta_copy(j, j).wait_recv()
        return carry

    own_meta.wait()
    lax.fori_loop(1, peers, hear, 0)

    def attend_chunk(c, carry):
        q_copy(c).wait_recv()
        f_column = pl.multiple_of(c * 2 * HD, 2 * HD)
        for g in range(GROUP):
            own_rows = pl.ds(g * rows, rows)
            column = pl.multiple_of(c * q_width + g * HD, HD)
            qs[0, own_rows, :] = turned(q_ref[:, pl.ds(column, HD)], cos_ref[0], sin_ref[0])
            qs[1, own_rows, :] = turned(partner_q[c, :, pl.ds(g * HD, HD)], cos_ref[1], sin_ref[1])
        own_key = turned(fresh_ref[:, pl.ds(f_column, HD)], cos_ref[0], sin_ref[0])
        own = lax.dot_general(own_key, qs[0], NT, preferred_element_type=jnp.float32)
        row_of = lax.broadcasted_iota(jnp.int32, (rows, lanes), 0)
        lane_of = lax.broadcasted_iota(jnp.int32, (rows, lanes), 1) % rows
        top[0] = jnp.sum(jnp.where(row_of == lane_of, own, 0.0), axis=0, keepdims=True)
        total[0] = jnp.ones((1, lanes), jnp.float32)
        own_value = fresh_ref[:, pl.ds(pl.multiple_of(f_column + HD, HD), HD)].astype(jnp.float32).T
        for g in range(GROUP):
            acc[0, :, pl.ds(g * rows, rows)] = own_value
        top[1] = jnp.full((1, lanes), NEG_START, jnp.float32)
        total[1] = jnp.zeros((1, lanes), jnp.float32)
        acc[1] = jnp.zeros((HD, lanes), jnp.float32)

        def attend(t, carry):
            j = lax.rem(me + peers - t, peers)

            @pl.when(t > 0)
            def _():
                kv_copy(c, j, j).wait_recv()

            @pl.when(t == 0)
            def _():
                own_kv(c).wait()

            req = metas[j, 0:1, :]
            offset = metas[j, 1:2, :]
            is_own = req == req_ref[0:1, :]
            is_partner = req == req_ref[1:2, :]
            pick0 = jnp.where(is_own, 1.0, 0.0).astype(jnp.bfloat16)
            pick1 = jnp.where(is_own, 0.0, 1.0).astype(jnp.bfloat16)
            query = qs[0] * pick0 + qs[1] * pick1
            wide_own = jnp.concatenate([is_own.astype(jnp.int32)] * GROUP, axis=1) > 0
            wide_partner = jnp.concatenate([is_partner.astype(jnp.int32)] * GROUP, axis=1) > 0
            wide_offset = jnp.concatenate([offset] * GROUP, axis=1)
            limit = jnp.where(wide_own, limit_ref[0], limit_ref[1]) - wide_offset
            keys = received[c, j, :, pl.ds(0, HD)]
            values = received[c, j, :, pl.ds(HD, HD)]
            scores = lax.dot_general(keys, query, NT, preferred_element_type=jnp.float32)
            token = lax.broadcasted_iota(jnp.int32, scores.shape, 0)
            scores = jnp.where(token < limit, scores, NEG_FILL)
            block_top = jnp.max(scores, axis=0, keepdims=True)
            weights = jnp.exp2((scores - block_top) * log_scale).astype(jnp.bfloat16)
            block_sum = jnp.sum(weights.astype(jnp.float32), axis=0, keepdims=True)
            block_out = lax.dot_general(values, weights, TN, preferred_element_type=jnp.float32)
            for side, chosen in enumerate((wide_own, wide_partner)):
                old_top = top[side]
                new_top = jnp.where(chosen, jnp.maximum(old_top, block_top), old_top)
                old_factor = jnp.exp2((old_top - new_top) * log_scale)
                new_factor = jnp.where(
                    chosen, jnp.exp2(jnp.where(chosen, block_top - new_top, 0.0) * log_scale), 0.0
                )
                top[side] = new_top
                total[side] = total[side] * old_factor + block_sum * new_factor
                acc[side] = acc[side] * old_factor + block_out * new_factor
            return carry

        lax.fori_loop(0, peers, attend, 0)
        o0[c] = acc[0] * (1.0 / total[0])
        lse0[c] = top[0] * scale + jnp.log(total[0])
        some = total[1] > 0.0
        safe = jnp.where(some, total[1], 1.0)
        o1[c] = (acc[1] * (1.0 / safe)).astype(jnp.bfloat16)
        sent_lse = jnp.where(some, top[1] * scale + jnp.log(safe), NEG_FILL)
        for g in range(GROUP):
            lse1[c, g : g + 1, :] = sent_lse[:, g * rows : (g + 1) * rows]
        l_copy(c).start()
        o_copy(c).start()
        return carry

    lax.fori_loop(0, heads, attend_chunk, 0)

    def merge_chunk(c, carry):
        l_copy(c).wait_recv()
        o_copy(c).wait_recv()
        base = lse0[c]
        other = jnp.concatenate([lse1_in[c, g : g + 1, :] for g in range(GROUP)], axis=1)
        larger = jnp.maximum(base, other)
        first, second = jnp.exp(base - larger), jnp.exp(other - larger)
        scaled = 1.0 / (first + second)
        joined = o0[c] * (first * scaled) + o1_in[c].astype(jnp.float32) * (second * scaled)
        for g in range(GROUP):
            column = pl.multiple_of(c * q_width + g * HD, HD)
            out_ref[:, pl.ds(column, HD)] = joined[:, g * rows : (g + 1) * rows].T.astype(out_ref.dtype)
        return carry

    lax.fori_loop(0, heads, merge_chunk, 0)

    def finish(c, carry):
        def sent_kv(t, carry):
            kv_copy(c, lax.rem(me + t, peers), me).wait_send()
            return carry

        lax.fori_loop(1, peers, sent_kv, 0)
        q_copy(c).wait_send()
        o_copy(c).wait_send()
        l_copy(c).wait_send()
        return carry

    lax.fori_loop(0, heads, finish, 0)

    def told(t, carry):
        meta_copy(lax.rem(me + t, peers), me).wait_send()
        return carry

    lax.fori_loop(1, peers, told, 0)


def shards(kv_store, block_order, lengths, row_positions, queries, fresh_rows):
    n_shard = lax.axis_size("shard")
    peers = n_shard // 2
    per_req = n_shard // REQS
    blk_dev, block_len, width = kv_store.shape
    heads = width // (per_req * 2 * HD)
    rows = queries.shape[0]
    lanes = rows * GROUP
    my_req = lax.axis_index("shard") // per_req
    req_ids = jnp.arange(REQS, dtype=jnp.int32)
    starts = jnp.sum(jnp.where(req_ids[None, :] < req_ids[:, None], lengths[None, :], 0), axis=1)
    dest = jnp.sum((block_order[:, None] >= starts[None, 1:]).astype(jnp.int32), axis=-1)
    offset = (block_order - lookup(starts, req_ids, dest)) * block_len
    pair_ids = jnp.arange(PAIRS, dtype=jnp.int32)
    slot_ids = jnp.arange(blk_dev, dtype=jnp.int32)
    for_pair = (dest % PAIRS)[None, :] == pair_ids[:, None]
    sel = jnp.sum(jnp.where(for_pair, slot_ids[None, :], 0), axis=1)
    pair_req = jnp.sum(jnp.where(for_pair, dest[None, :] + 1, 0), axis=1) - 1
    pair_offset = jnp.sum(jnp.where(for_pair, offset[None, :], 0), axis=1)
    row_ids = jnp.arange(8, dtype=jnp.int32)
    meta = jnp.broadcast_to(
        jnp.where(row_ids[None, :] == 0, pair_req[:, None], pair_offset[:, None])[:, :, None], (PAIRS, 8, HD)
    )
    block_cos, block_sin = turn_tables(offset[:, None])
    other_req = (my_req + PAIRS) % REQS
    both = jnp.stack(
        [
            lax.dynamic_index_in_dim(row_positions, my_req, 0, keepdims=False),
            lax.dynamic_index_in_dim(row_positions, other_req, 0, keepdims=False),
        ]
    )
    row_cos, row_sin = turn_tables(both)
    limits = jnp.tile(both, (1, GROUP))[:, None, :]
    reqs = jnp.broadcast_to(jnp.where(row_ids == 0, my_req, other_req)[:, None], (8, HD))
    vmem = pl.BlockSpec(memory_space=pltpu.VMEM)
    dma = pltpu.SemaphoreType.DMA
    return pl.pallas_call(
        functools.partial(whole_kernel, n_shard, 1.0 / math.sqrt(HD)),
        out_shape=jax.ShapeDtypeStruct(queries.shape, jnp.bfloat16),
        in_specs=[pl.BlockSpec(memory_space=pltpu.SMEM)] + [vmem] * 10,
        out_specs=vmem,
        scratch_shapes=[
            pltpu.VMEM((heads, peers, block_len, 2 * HD), jnp.bfloat16),
            pltpu.VMEM((heads, peers, block_len, 2 * HD), jnp.bfloat16),
            pltpu.VMEM((peers, 8, HD), jnp.int32),
            pltpu.VMEM((heads, rows, GROUP * HD), jnp.bfloat16),
            pltpu.VMEM((2, lanes, HD), jnp.bfloat16),
            pltpu.VMEM((2, 1, lanes), jnp.float32),
            pltpu.VMEM((2, 1, lanes), jnp.float32),
            pltpu.VMEM((2, HD, lanes), jnp.float32),
            pltpu.VMEM((heads, HD, lanes), jnp.float32),
            pltpu.VMEM((heads, 1, lanes), jnp.float32),
            pltpu.VMEM((heads, HD, lanes), jnp.bfloat16),
            pltpu.VMEM((heads, GROUP, rows), jnp.float32),
            pltpu.VMEM((heads, HD, lanes), jnp.bfloat16),
            pltpu.VMEM((heads, GROUP, rows), jnp.float32),
            dma((heads, peers)),
            dma((heads, peers)),
            dma((peers,)),
            dma((peers,)),
            dma((heads,)),
            dma((heads,)),
            dma((heads,)),
            dma((heads,)),
            dma((heads,)),
            dma((heads,)),
            dma((heads + 1,)),
        ],
        compiler_params=pltpu.CompilerParams(
            collective_id=0, has_side_effects=True, vmem_limit_bytes=44 << 20
        ),
        cost_estimate=pl.CostEstimate(
            flops=4 * heads * peers * block_len * lanes * HD,
            bytes_accessed=8 << 20,
            transcendentals=heads * peers * block_len * lanes,
        ),
        name="whole",
    )(sel, kv_store, block_cos, block_sin, meta, queries, fresh_rows, row_cos, row_sin, limits, reqs)


def solution(mesh):
    in_specs = (
        P(("groups", "shard"), None, None),
        P(("groups", "shard")),
        P("groups"),
        P("groups", None),
        P("groups", "shard"),
        P("groups", "shard"),
    )
    out_specs = P("groups", "shard")
    return jax.shard_map(shards, mesh=mesh, in_specs=in_specs, out_specs=out_specs, check_vma=False)
```

```python
import functools
import math

import jax
import jax.numpy as jnp
from jax import lax
from jax.experimental import pallas as pl
from jax.experimental.pallas import tpu as pltpu
from jax.sharding import PartitionSpec as P

QH = 64
KVH = 8
HD = 128
REQS = 8
GROUP = QH // KVH
PAIRS = REQS // 2

ROPE_BASE = 500000.0
NEG_FILL = -1e30
NEG_START = -1e29
LOG2E = 1.4426950408889634
NT = (((1,), (1,)), ((), ()))
TN = (((0,), (0,)), ((), ()))


def frequency_lanes():
    lane = lax.rem(lax.broadcasted_iota(jnp.int32, (1, HD), 1), HD // 2)
    return jnp.exp(-math.log(ROPE_BASE) * lane.astype(jnp.float32) / (HD // 2))


def turn_tables(positions):
    angle = positions.astype(jnp.float32) * frequency_lanes()
    lower = lax.broadcasted_iota(jnp.int32, angle.shape, 1) < HD // 2
    sine = jnp.sin(angle)
    return jnp.cos(angle), jnp.where(lower, -sine, sine)


def turned(x, cosine, sine):
    x = x.astype(jnp.float32)
    return (x * cosine + pltpu.roll(x, HD // 2, 1) * sine).astype(jnp.bfloat16)


def whole_kernel(
    n,
    scale,
    order_ref,
    lengths_ref,
    positions_ref,
    kv_hbm,
    q_hbm,
    fresh_hbm,
    out_ref,
    kv_ref,
    q_ref,
    fresh_ref,
    sel_ref,
    bcos_ref,
    bsin_ref,
    meta_ref,
    cos_ref,
    sin_ref,
    sent,
    received,
    metas,
    partner_q,
    qs,
    top,
    total,
    acc,
    o0,
    lse0,
    o1,
    lse1,
    o1_in,
    lse1_in,
    kv_send,
    kv_recv,
    meta_send,
    meta_recv,
    q_send,
    q_recv,
    o_send,
    o_recv,
    l_send,
    l_recv,
    local_sem,
    load_sem,
):
    heads, peers, block_len, _ = sent.shape
    rows = q_ref.shape[0]
    lanes = rows * GROUP
    q_width = GROUP * HD
    per_req = n // REQS
    device = lax.axis_index("shard")
    me = lax.rem(device, peers)
    first_peer = device - me
    partner = lax.rem(device + peers, n)
    log_scale = scale * LOG2E

    def remote(src, dst, send, recv, target):
        return pltpu.make_async_remote_copy(
            src_ref=src,
            dst_ref=dst,
            send_sem=send,
            recv_sem=recv,
            device_id={"shard": target},
            device_id_type=pl.DeviceIdType.MESH,
        )

    def kv_copy(c, i, slot):
        return remote(sent.at[c, i], received.at[c, slot], kv_send.at[c, i], kv_recv.at[c, slot], first_peer + i)

    def meta_copy(i, slot):
        return remote(
            meta_ref.at[i // per_req], metas.at[slot], meta_send.at[i], meta_recv.at[slot], first_peer + i
        )

    def q_copy(c):
        columns = pl.ds(pl.multiple_of(c * q_width, q_width), q_width)
        return remote(q_hbm.at[:, columns], partner_q.at[c], q_send.at[c], q_recv.at[c], partner)

    def o_copy(c):
        return remote(o1.at[c], o1_in.at[c], o_send.at[c], o_recv.at[c], partner)

    def l_copy(c):
        return remote(lse1.at[c], lse1_in.at[c], l_send.at[c], l_recv.at[c], partner)

    def own_kv(c):
        return pltpu.make_async_copy(sent.at[c, me], received.at[c, me], local_sem.at[c])

    loads = [
        pltpu.make_async_copy(hbm, here, load_sem.at[i])
        for i, (hbm, here) in enumerate(((kv_hbm, kv_ref), (q_hbm, q_ref), (fresh_hbm, fresh_ref)))
    ]
    for load in loads:
        load.start()

    barrier = pltpu.get_barrier_semaphore()
    pl.semaphore_signal(barrier, inc=1, device_id={"shard": partner}, device_id_type=pl.DeviceIdType.MESH)

    def greet(t, carry):
        pl.semaphore_signal(
            barrier,
            inc=1,
            device_id={"shard": first_peer + lax.rem(me + t, peers)},
            device_id_type=pl.DeviceIdType.MESH,
        )
        return carry

    lax.fori_loop(1, peers, greet, 0)
    my_req = device // per_req
    other_req = lax.rem(my_req + PAIRS, REQS)
    reqs, offsets = [], []
    for b in range(order_ref.shape[0]):
        block = order_ref[b]
        start, req, own_start = jnp.int32(0), jnp.int32(-1), jnp.int32(0)
        for r in range(REQS):
            inside = block >= start
            req = jnp.where(inside, r, req)
            own_start = jnp.where(inside, start, own_start)
            start = start + lengths_ref[r]
        offset = (block - own_start) * block_len
        reqs.append(req)
        offsets.append(offset)
        cosine, sine = turn_tables(jnp.full((1, HD), offset, jnp.int32))
        bcos_ref[b] = cosine
        bsin_ref[b] = sine
    row_of_8 = lax.broadcasted_iota(jnp.int32, (8, HD), 0)
    for p in range(PAIRS):
        sel, pair_req, pair_offset = jnp.int32(0), jnp.int32(-1), jnp.int32(0)
        for b, (req, offset) in enumerate(zip(reqs, offsets)):
            match = lax.rem(req, PAIRS) == p
            sel = jnp.where(match, b, sel)
            pair_req = jnp.where(match, req, pair_req)
            pair_offset = jnp.where(match, offset, pair_offset)
        sel_ref[p] = sel
        meta_ref[p] = jnp.where(row_of_8 == 0, pair_req, pair_offset)

    pl.semaphore_wait(barrier, peers)
    q_copy(0).start()
    loads[0].wait()

    own_meta = pltpu.make_async_copy(meta_ref.at[me // per_req], metas.at[me], local_sem.at[heads])
    own_meta.start()

    def tell(t, carry):
        meta_copy(lax.rem(me + t, peers), me).start()
        return carry

    lax.fori_loop(1, peers, tell, 0)

    def pack_chunk(c, carry):
        @pl.when(c > 0)
        def _():
            q_copy(c).start()

        def pack(t, carry):
            i = lax.rem(me + t, peers)
            pair, group = i // per_req, lax.rem(i, per_req)
            sel = sel_ref[pair]
            column = pl.multiple_of((group * heads + c) * 2 * HD, 2 * HD)
            key = kv_ref[sel, :, pl.ds(column, HD)]
            sent[c, i, :, pl.ds(0, HD)] = turned(key, bcos_ref[sel], bsin_ref[sel])
            sent[c, i, :, pl.ds(HD, HD)] = kv_ref[sel, :, pl.ds(pl.multiple_of(column + HD, HD), HD)]

            @pl.when(t > 0)
            def _():
                kv_copy(c, i, me).start()

            @pl.when(t == 0)
            def _():
                own_kv(c).start()

            return carry

        return lax.fori_loop(0, peers, pack, carry)

    lax.fori_loop(0, heads, pack_chunk, 0)

    def hear(t, carry):
        j = lax.rem(me + t, peers)
        meta_copy(j, j).wait_recv()
        return carry

    limits = []
    for side, req in enumerate((my_req, other_req)):
        positions = positions_ref[pl.ds(req, 1), :]
        limits.append(jnp.concatenate([positions] * GROUP, axis=1))
        column = jnp.broadcast_to(positions.astype(jnp.float32), (HD, rows)).T
        cosine, sine = turn_tables(column)
        cos_ref[side] = cosine
        sin_ref[side] = sine
    loads[1].wait()
    loads[2].wait()
    own_meta.wait()
    lax.fori_loop(1, peers, hear, 0)

    def attend_chunk(c, carry):
        q_copy(c).wait_recv()
        f_column = pl.multiple_of(c * 2 * HD, 2 * HD)
        for g in range(GROUP):
            own_rows = pl.ds(g * rows, rows)
            column = pl.multiple_of(c * q_width + g * HD, HD)
            qs[0, own_rows, :] = turned(q_ref[:, pl.ds(column, HD)], cos_ref[0], sin_ref[0])
            qs[1, own_rows, :] = turned(partner_q[c, :, pl.ds(g * HD, HD)], cos_ref[1], sin_ref[1])
        own_key = turned(fresh_ref[:, pl.ds(f_column, HD)], cos_ref[0], sin_ref[0])
        own = lax.dot_general(own_key, qs[0], NT, preferred_element_type=jnp.float32)
        row_of = lax.broadcasted_iota(jnp.int32, (rows, lanes), 0)
        lane_of = lax.broadcasted_iota(jnp.int32, (rows, lanes), 1) % rows
        top[0] = jnp.sum(jnp.where(row_of == lane_of, own, 0.0), axis=0, keepdims=True)
        total[0] = jnp.ones((1, lanes), jnp.float32)
        own_value = fresh_ref[:, pl.ds(pl.multiple_of(f_column + HD, HD), HD)].astype(jnp.float32).T
        for g in range(GROUP):
            acc[0, :, pl.ds(g * rows, rows)] = own_value
        top[1] = jnp.full((1, lanes), NEG_START, jnp.float32)
        total[1] = jnp.zeros((1, lanes), jnp.float32)
        acc[1] = jnp.zeros((HD, lanes), jnp.float32)

        def attend(t, carry):
            j = lax.rem(me + peers - t, peers)

            @pl.when(t > 0)
            def _():
                kv_copy(c, j, j).wait_recv()

            @pl.when(t == 0)
            def _():
                own_kv(c).wait()

            req = metas[j, 0:1, :]
            offset = metas[j, 1:2, :]
            is_own = req == my_req
            is_partner = req == other_req
            pick0 = jnp.where(is_own, 1.0, 0.0).astype(jnp.bfloat16)
            pick1 = jnp.where(is_own, 0.0, 1.0).astype(jnp.bfloat16)
            query = qs[0] * pick0 + qs[1] * pick1
            wide_own = jnp.concatenate([is_own.astype(jnp.int32)] * GROUP, axis=1) > 0
            wide_partner = jnp.concatenate([is_partner.astype(jnp.int32)] * GROUP, axis=1) > 0
            wide_offset = jnp.concatenate([offset] * GROUP, axis=1)
            limit = jnp.where(wide_own, limits[0], limits[1]) - wide_offset
            keys = received[c, j, :, pl.ds(0, HD)]
            values = received[c, j, :, pl.ds(HD, HD)]
            scores = lax.dot_general(keys, query, NT, preferred_element_type=jnp.float32)
            token = lax.broadcasted_iota(jnp.int32, scores.shape, 0)
            scores = jnp.where(token < limit, scores, NEG_FILL)
            block_top = jnp.max(scores, axis=0, keepdims=True)
            weights = jnp.exp2((scores - block_top) * log_scale).astype(jnp.bfloat16)
            block_sum = jnp.sum(weights.astype(jnp.float32), axis=0, keepdims=True)
            block_out = lax.dot_general(values, weights, TN, preferred_element_type=jnp.float32)
            for side, chosen in enumerate((wide_own, wide_partner)):
                old_top = top[side]
                new_top = jnp.where(chosen, jnp.maximum(old_top, block_top), old_top)
                old_factor = jnp.exp2((old_top - new_top) * log_scale)
                new_factor = jnp.where(
                    chosen, jnp.exp2(jnp.where(chosen, block_top - new_top, 0.0) * log_scale), 0.0
                )
                top[side] = new_top
                total[side] = total[side] * old_factor + block_sum * new_factor
                acc[side] = acc[side] * old_factor + block_out * new_factor
            return carry

        lax.fori_loop(0, peers, attend, 0)
        o0[c] = acc[0] * (1.0 / total[0])
        lse0[c] = top[0] * scale + jnp.log(total[0])
        some = total[1] > 0.0
        safe = jnp.where(some, total[1], 1.0)
        o1[c] = (acc[1] * (1.0 / safe)).astype(jnp.bfloat16)
        sent_lse = jnp.where(some, top[1] * scale + jnp.log(safe), NEG_FILL)
        for g in range(GROUP):
            lse1[c, g : g + 1, :] = sent_lse[:, g * rows : (g + 1) * rows]
        l_copy(c).start()
        o_copy(c).start()
        return carry

    lax.fori_loop(0, heads, attend_chunk, 0)

    def merge_chunk(c, carry):
        l_copy(c).wait_recv()
        o_copy(c).wait_recv()
        base = lse0[c]
        other = jnp.concatenate([lse1_in[c, g : g + 1, :] for g in range(GROUP)], axis=1)
        larger = jnp.maximum(base, other)
        first, second = jnp.exp(base - larger), jnp.exp(other - larger)
        scaled = 1.0 / (first + second)
        joined = o0[c] * (first * scaled) + o1_in[c].astype(jnp.float32) * (second * scaled)
        for g in range(GROUP):
            column = pl.multiple_of(c * q_width + g * HD, HD)
            out_ref[:, pl.ds(column, HD)] = joined[:, g * rows : (g + 1) * rows].T.astype(out_ref.dtype)
        return carry

    lax.fori_loop(0, heads, merge_chunk, 0)

    def finish(c, carry):
        def sent_kv(t, carry):
            kv_copy(c, lax.rem(me + t, peers), me).wait_send()
            return carry

        lax.fori_loop(1, peers, sent_kv, 0)
        q_copy(c).wait_send()
        o_copy(c).wait_send()
        l_copy(c).wait_send()
        return carry

    lax.fori_loop(0, heads, finish, 0)

    def told(t, carry):
        meta_copy(lax.rem(me + t, peers), me).wait_send()
        return carry

    lax.fori_loop(1, peers, told, 0)


def shards(kv_store, block_order, lengths, row_positions, queries, fresh_rows):
    n_shard = lax.axis_size("shard")
    peers = n_shard // 2
    per_req = n_shard // REQS
    blk_dev, block_len, width = kv_store.shape
    heads = width // (per_req * 2 * HD)
    rows = queries.shape[0]
    lanes = rows * GROUP
    vmem = pl.BlockSpec(memory_space=pltpu.VMEM)
    smem = pl.BlockSpec(memory_space=pltpu.SMEM)
    anywhere = pl.BlockSpec(memory_space=pl.ANY)
    dma = pltpu.SemaphoreType.DMA
    return pl.pallas_call(
        functools.partial(whole_kernel, n_shard, 1.0 / math.sqrt(HD)),
        out_shape=jax.ShapeDtypeStruct(queries.shape, jnp.bfloat16),
        in_specs=[smem, smem, vmem, anywhere, anywhere, anywhere],
        out_specs=vmem,
        scratch_shapes=[
            pltpu.VMEM(kv_store.shape, kv_store.dtype),
            pltpu.VMEM(queries.shape, queries.dtype),
            pltpu.VMEM(fresh_rows.shape, fresh_rows.dtype),
            pltpu.SMEM((PAIRS,), jnp.int32),
            pltpu.VMEM((blk_dev, 1, HD), jnp.float32),
            pltpu.VMEM((blk_dev, 1, HD), jnp.float32),
            pltpu.VMEM((PAIRS, 8, HD), jnp.int32),
            pltpu.VMEM((2, rows, HD), jnp.float32),
            pltpu.VMEM((2, rows, HD), jnp.float32),
            pltpu.VMEM((heads, peers, block_len, 2 * HD), jnp.bfloat16),
            pltpu.VMEM((heads, peers, block_len, 2 * HD), jnp.bfloat16),
            pltpu.VMEM((peers, 8, HD), jnp.int32),
            pltpu.VMEM((heads, rows, GROUP * HD), jnp.bfloat16),
            pltpu.VMEM((2, lanes, HD), jnp.bfloat16),
            pltpu.VMEM((2, 1, lanes), jnp.float32),
            pltpu.VMEM((2, 1, lanes), jnp.float32),
            pltpu.VMEM((2, HD, lanes), jnp.float32),
            pltpu.VMEM((heads, HD, lanes), jnp.float32),
            pltpu.VMEM((heads, 1, lanes), jnp.float32),
            pltpu.VMEM((heads, HD, lanes), jnp.bfloat16),
            pltpu.VMEM((heads, GROUP, rows), jnp.float32),
            pltpu.VMEM((heads, HD, lanes), jnp.bfloat16),
            pltpu.VMEM((heads, GROUP, rows), jnp.float32),
            dma((heads, peers)),
            dma((heads, peers)),
            dma((peers,)),
            dma((peers,)),
            dma((heads,)),
            dma((heads,)),
            dma((heads,)),
            dma((heads,)),
            dma((heads,)),
            dma((heads,)),
            dma((heads + 1,)),
            dma((3,)),
        ],
        compiler_params=pltpu.CompilerParams(
            collective_id=0, has_side_effects=True, vmem_limit_bytes=60 << 20
        ),
        cost_estimate=pl.CostEstimate(
            flops=4 * heads * peers * block_len * lanes * HD,
            bytes_accessed=8 << 20,
            transcendentals=heads * peers * block_len * lanes,
        ),
        name="whole",
    )(block_order, lengths, row_positions, kv_store, queries, fresh_rows)


def solution(mesh):
    in_specs = (
        P(("groups", "shard"), None, None),
        P(("groups", "shard")),
        P("groups"),
        P("groups", None),
        P("groups", "shard"),
        P("groups", "shard"),
    )
    out_specs = P("groups", "shard")
    return jax.shard_map(shards, mesh=mesh, in_specs=in_specs, out_specs=out_specs, check_vma=False)
```

```python
import functools
import math

import jax
import jax.numpy as jnp
from jax import lax
from jax.experimental import pallas as pl
from jax.experimental.pallas import tpu as pltpu
from jax.sharding import PartitionSpec as P

QH = 64
KVH = 8
HD = 128
REQS = 8
GROUP = QH // KVH
PAIRS = REQS // 2

ROPE_BASE = 500000.0
NEG_FILL = -1e30
NEG_START = -1e29
LOG2E = 1.4426950408889634
NT = (((1,), (1,)), ((), ()))
TN = (((0,), (0,)), ((), ()))


def frequency_lanes():
    lane = lax.rem(lax.broadcasted_iota(jnp.int32, (1, HD), 1), HD // 2)
    return jnp.exp(-math.log(ROPE_BASE) * lane.astype(jnp.float32) / (HD // 2))


def turn_tables(positions):
    angle = positions.astype(jnp.float32) * frequency_lanes()
    lower = lax.broadcasted_iota(jnp.int32, angle.shape, 1) < HD // 2
    sine = jnp.sin(angle)
    return jnp.cos(angle), jnp.where(lower, -sine, sine)


def turned(x, cosine, sine):
    x = x.astype(jnp.float32)
    return (x * cosine + pltpu.roll(x, HD // 2, 1) * sine).astype(jnp.bfloat16)


def whole_kernel(
    n,
    scale,
    order_ref,
    lengths_ref,
    positions_ref,
    kv_hbm,
    q_hbm,
    fresh_hbm,
    out_ref,
    kv_ref,
    q_ref,
    fresh_ref,
    sel_ref,
    bcos_ref,
    bsin_ref,
    meta_ref,
    cos_ref,
    sin_ref,
    sent,
    received,
    metas,
    partner_q,
    qs,
    top,
    total,
    acc,
    o0,
    lse0,
    o1,
    lse1,
    o1_in,
    lse1_in,
    kv_send,
    kv_recv,
    meta_send,
    meta_recv,
    q_send,
    q_recv,
    o_send,
    o_recv,
    l_send,
    l_recv,
    local_sem,
    load_sem,
):
    heads, peers, block_len, _ = sent.shape
    rows = q_ref.shape[0]
    lanes = rows * GROUP
    q_width = GROUP * HD
    per_req = n // REQS
    device = lax.axis_index("shard")
    me = lax.rem(device, peers)
    first_peer = device - me
    partner = lax.rem(device + peers, n)
    log_scale = scale * LOG2E

    def remote(src, dst, send, recv, target):
        return pltpu.make_async_remote_copy(
            src_ref=src,
            dst_ref=dst,
            send_sem=send,
            recv_sem=recv,
            device_id={"shard": target},
            device_id_type=pl.DeviceIdType.MESH,
        )

    def kv_copy(c, i, slot):
        return remote(sent.at[c, i], received.at[c, slot], kv_send.at[c, i], kv_recv.at[c, slot], first_peer + i)

    def meta_copy(i, slot):
        return remote(
            meta_ref.at[i // per_req], metas.at[slot], meta_send.at[i], meta_recv.at[slot], first_peer + i
        )

    def q_copy(c):
        columns = pl.ds(pl.multiple_of(c * q_width, q_width), q_width)
        return remote(q_hbm.at[:, columns], partner_q.at[c], q_send.at[c], q_recv.at[c], partner)

    def o_copy(c):
        return remote(o1.at[c], o1_in.at[c], o_send.at[c], o_recv.at[c], partner)

    def l_copy(c):
        return remote(lse1.at[c], lse1_in.at[c], l_send.at[c], l_recv.at[c], partner)

    def own_kv(c):
        return pltpu.make_async_copy(sent.at[c, me], received.at[c, me], local_sem.at[c])

    loads = [
        pltpu.make_async_copy(hbm, here, load_sem.at[i])
        for i, (hbm, here) in enumerate(((kv_hbm, kv_ref), (q_hbm, q_ref), (fresh_hbm, fresh_ref)))
    ]
    for load in loads:
        load.start()

    barrier = pltpu.get_barrier_semaphore()
    pl.semaphore_signal(barrier, inc=1, device_id={"shard": partner}, device_id_type=pl.DeviceIdType.MESH)

    def greet(t, carry):
        pl.semaphore_signal(
            barrier,
            inc=1,
            device_id={"shard": first_peer + lax.rem(me + t, peers)},
            device_id_type=pl.DeviceIdType.MESH,
        )
        return carry

    lax.fori_loop(1, peers, greet, 0)
    pl.semaphore_wait(barrier, peers)

    def ask(c, carry):
        q_copy(c).start()
        return carry

    lax.fori_loop(0, heads, ask, 0)
    my_req = device // per_req
    other_req = lax.rem(my_req + PAIRS, REQS)
    reqs, offsets = [], []
    for b in range(order_ref.shape[0]):
        block = order_ref[b]
        start, req, own_start = jnp.int32(0), jnp.int32(-1), jnp.int32(0)
        for r in range(REQS):
            inside = block >= start
            req = jnp.where(inside, r, req)
            own_start = jnp.where(inside, start, own_start)
            start = start + lengths_ref[r]
        offset = (block - own_start) * block_len
        reqs.append(req)
        offsets.append(offset)
        cosine, sine = turn_tables(jnp.full((1, HD), offset, jnp.int32))
        bcos_ref[b] = cosine
        bsin_ref[b] = sine
    row_of_8 = lax.broadcasted_iota(jnp.int32, (8, HD), 0)
    for p in range(PAIRS):
        sel, pair_req, pair_offset = jnp.int32(0), jnp.int32(-1), jnp.int32(0)
        for b, (req, offset) in enumerate(zip(reqs, offsets)):
            match = lax.rem(req, PAIRS) == p
            sel = jnp.where(match, b, sel)
            pair_req = jnp.where(match, req, pair_req)
            pair_offset = jnp.where(match, offset, pair_offset)
        sel_ref[p] = sel
        meta_ref[p] = jnp.where(row_of_8 == 0, pair_req, pair_offset)

    loads[0].wait()

    own_meta = pltpu.make_async_copy(meta_ref.at[me // per_req], metas.at[me], local_sem.at[heads])
    own_meta.start()

    def tell(t, carry):
        meta_copy(lax.rem(me + t, peers), me).start()
        return carry

    lax.fori_loop(1, peers, tell, 0)

    def pack_chunk(c, carry):
        def pack(t, carry):
            i = lax.rem(me + t, peers)
            pair, group = i // per_req, lax.rem(i, per_req)
            sel = sel_ref[pair]
            column = pl.multiple_of((group * heads + c) * 2 * HD, 2 * HD)
            key = kv_ref[sel, :, pl.ds(column, HD)]
            sent[c, i, :, pl.ds(0, HD)] = turned(key, bcos_ref[sel], bsin_ref[sel])
            sent[c, i, :, pl.ds(HD, HD)] = kv_ref[sel, :, pl.ds(pl.multiple_of(column + HD, HD), HD)]

            @pl.when(t > 0)
            def _():
                kv_copy(c, i, me).start()

            @pl.when(t == 0)
            def _():
                own_kv(c).start()

            return carry

        return lax.fori_loop(0, peers, pack, carry)

    lax.fori_loop(0, heads, pack_chunk, 0)

    def hear(t, carry):
        j = lax.rem(me + t, peers)
        meta_copy(j, j).wait_recv()
        return carry

    limits = []
    for side, req in enumerate((my_req, other_req)):
        positions = positions_ref[pl.ds(req, 1), :]
        limits.append(jnp.concatenate([positions] * GROUP, axis=1))
        column = jnp.broadcast_to(positions.astype(jnp.float32), (HD, rows)).T
        cosine, sine = turn_tables(column)
        cos_ref[side] = cosine
        sin_ref[side] = sine
    loads[1].wait()
    loads[2].wait()
    own_meta.wait()
    lax.fori_loop(1, peers, hear, 0)

    def attend_chunk(c, carry):
        q_copy(c).wait_recv()
        f_column = pl.multiple_of(c * 2 * HD, 2 * HD)
        for g in range(GROUP):
            own_rows = pl.ds(g * rows, rows)
            column = pl.multiple_of(c * q_width + g * HD, HD)
            qs[0, own_rows, :] = turned(q_ref[:, pl.ds(column, HD)], cos_ref[0], sin_ref[0])
            qs[1, own_rows, :] = turned(partner_q[c, :, pl.ds(g * HD, HD)], cos_ref[1], sin_ref[1])
        own_key = turned(fresh_ref[:, pl.ds(f_column, HD)], cos_ref[0], sin_ref[0])
        own = lax.dot_general(own_key, qs[0], NT, preferred_element_type=jnp.float32)
        row_of = lax.broadcasted_iota(jnp.int32, (rows, lanes), 0)
        lane_of = lax.broadcasted_iota(jnp.int32, (rows, lanes), 1) % rows
        top[0] = jnp.sum(jnp.where(row_of == lane_of, own, 0.0), axis=0, keepdims=True)
        total[0] = jnp.ones((1, lanes), jnp.float32)
        own_value = fresh_ref[:, pl.ds(pl.multiple_of(f_column + HD, HD), HD)].astype(jnp.float32).T
        for g in range(GROUP):
            acc[0, :, pl.ds(g * rows, rows)] = own_value
        top[1] = jnp.full((1, lanes), NEG_START, jnp.float32)
        total[1] = jnp.zeros((1, lanes), jnp.float32)
        acc[1] = jnp.zeros((HD, lanes), jnp.float32)

        def attend(t, carry):
            j = lax.rem(me + peers - t, peers)

            @pl.when(t > 0)
            def _():
                kv_copy(c, j, j).wait_recv()

            @pl.when(t == 0)
            def _():
                own_kv(c).wait()

            req = metas[j, 0:1, :]
            offset = metas[j, 1:2, :]
            is_own = req == my_req
            is_partner = req == other_req
            pick0 = jnp.where(is_own, 1.0, 0.0).astype(jnp.bfloat16)
            pick1 = jnp.where(is_own, 0.0, 1.0).astype(jnp.bfloat16)
            query = qs[0] * pick0 + qs[1] * pick1
            wide_own = jnp.concatenate([is_own.astype(jnp.int32)] * GROUP, axis=1) > 0
            wide_partner = jnp.concatenate([is_partner.astype(jnp.int32)] * GROUP, axis=1) > 0
            wide_offset = jnp.concatenate([offset] * GROUP, axis=1)
            limit = jnp.where(wide_own, limits[0], limits[1]) - wide_offset
            keys = received[c, j, :, pl.ds(0, HD)]
            values = received[c, j, :, pl.ds(HD, HD)]
            scores = lax.dot_general(keys, query, NT, preferred_element_type=jnp.float32)
            token = lax.broadcasted_iota(jnp.int32, scores.shape, 0)
            scores = jnp.where(token < limit, scores, NEG_FILL)
            block_top = jnp.max(scores, axis=0, keepdims=True)
            weights = jnp.exp2((scores - block_top) * log_scale).astype(jnp.bfloat16)
            block_sum = jnp.sum(weights.astype(jnp.float32), axis=0, keepdims=True)
            block_out = lax.dot_general(values, weights, TN, preferred_element_type=jnp.float32)
            for side, chosen in enumerate((wide_own, wide_partner)):
                old_top = top[side]
                new_top = jnp.where(chosen, jnp.maximum(old_top, block_top), old_top)
                old_factor = jnp.exp2((old_top - new_top) * log_scale)
                new_factor = jnp.where(
                    chosen, jnp.exp2(jnp.where(chosen, block_top - new_top, 0.0) * log_scale), 0.0
                )
                top[side] = new_top
                total[side] = total[side] * old_factor + block_sum * new_factor
                acc[side] = acc[side] * old_factor + block_out * new_factor
            return carry

        lax.fori_loop(0, peers, attend, 0)
        o0[c] = acc[0] * (1.0 / total[0])
        lse0[c] = top[0] * scale + jnp.log(total[0])
        some = total[1] > 0.0
        safe = jnp.where(some, total[1], 1.0)
        o1[c] = (acc[1] * (1.0 / safe)).astype(jnp.bfloat16)
        sent_lse = jnp.where(some, top[1] * scale + jnp.log(safe), NEG_FILL)
        for g in range(GROUP):
            lse1[c, g : g + 1, :] = sent_lse[:, g * rows : (g + 1) * rows]
        l_copy(c).start()
        o_copy(c).start()
        return carry

    lax.fori_loop(0, heads, attend_chunk, 0)

    def merge_chunk(c, carry):
        l_copy(c).wait_recv()
        o_copy(c).wait_recv()
        base = lse0[c]
        other = jnp.concatenate([lse1_in[c, g : g + 1, :] for g in range(GROUP)], axis=1)
        larger = jnp.maximum(base, other)
        first, second = jnp.exp(base - larger), jnp.exp(other - larger)
        scaled = 1.0 / (first + second)
        joined = o0[c] * (first * scaled) + o1_in[c].astype(jnp.float32) * (second * scaled)
        for g in range(GROUP):
            column = pl.multiple_of(c * q_width + g * HD, HD)
            out_ref[:, pl.ds(column, HD)] = joined[:, g * rows : (g + 1) * rows].T.astype(out_ref.dtype)
        return carry

    lax.fori_loop(0, heads, merge_chunk, 0)

    def finish(c, carry):
        def sent_kv(t, carry):
            kv_copy(c, lax.rem(me + t, peers), me).wait_send()
            return carry

        lax.fori_loop(1, peers, sent_kv, 0)
        q_copy(c).wait_send()
        o_copy(c).wait_send()
        l_copy(c).wait_send()
        return carry

    lax.fori_loop(0, heads, finish, 0)

    def told(t, carry):
        meta_copy(lax.rem(me + t, peers), me).wait_send()
        return carry

    lax.fori_loop(1, peers, told, 0)


def shards(kv_store, block_order, lengths, row_positions, queries, fresh_rows):
    n_shard = lax.axis_size("shard")
    peers = n_shard // 2
    per_req = n_shard // REQS
    blk_dev, block_len, width = kv_store.shape
    heads = width // (per_req * 2 * HD)
    rows = queries.shape[0]
    lanes = rows * GROUP
    vmem = pl.BlockSpec(memory_space=pltpu.VMEM)
    smem = pl.BlockSpec(memory_space=pltpu.SMEM)
    anywhere = pl.BlockSpec(memory_space=pl.ANY)
    dma = pltpu.SemaphoreType.DMA
    return pl.pallas_call(
        functools.partial(whole_kernel, n_shard, 1.0 / math.sqrt(HD)),
        out_shape=jax.ShapeDtypeStruct(queries.shape, jnp.bfloat16),
        in_specs=[smem, smem, vmem, anywhere, anywhere, anywhere],
        out_specs=vmem,
        scratch_shapes=[
            pltpu.VMEM(kv_store.shape, kv_store.dtype),
            pltpu.VMEM(queries.shape, queries.dtype),
            pltpu.VMEM(fresh_rows.shape, fresh_rows.dtype),
            pltpu.SMEM((PAIRS,), jnp.int32),
            pltpu.VMEM((blk_dev, 1, HD), jnp.float32),
            pltpu.VMEM((blk_dev, 1, HD), jnp.float32),
            pltpu.VMEM((PAIRS, 8, HD), jnp.int32),
            pltpu.VMEM((2, rows, HD), jnp.float32),
            pltpu.VMEM((2, rows, HD), jnp.float32),
            pltpu.VMEM((heads, peers, block_len, 2 * HD), jnp.bfloat16),
            pltpu.VMEM((heads, peers, block_len, 2 * HD), jnp.bfloat16),
            pltpu.VMEM((peers, 8, HD), jnp.int32),
            pltpu.VMEM((heads, rows, GROUP * HD), jnp.bfloat16),
            pltpu.VMEM((2, lanes, HD), jnp.bfloat16),
            pltpu.VMEM((2, 1, lanes), jnp.float32),
            pltpu.VMEM((2, 1, lanes), jnp.float32),
            pltpu.VMEM((2, HD, lanes), jnp.float32),
            pltpu.VMEM((heads, HD, lanes), jnp.float32),
            pltpu.VMEM((heads, 1, lanes), jnp.float32),
            pltpu.VMEM((heads, HD, lanes), jnp.bfloat16),
            pltpu.VMEM((heads, GROUP, rows), jnp.float32),
            pltpu.VMEM((heads, HD, lanes), jnp.bfloat16),
            pltpu.VMEM((heads, GROUP, rows), jnp.float32),
            dma((heads, peers)),
            dma((heads, peers)),
            dma((peers,)),
            dma((peers,)),
            dma((heads,)),
            dma((heads,)),
            dma((heads,)),
            dma((heads,)),
            dma((heads,)),
            dma((heads,)),
            dma((heads + 1,)),
            dma((3,)),
        ],
        compiler_params=pltpu.CompilerParams(
            collective_id=0, has_side_effects=True, vmem_limit_bytes=60 << 20
        ),
        cost_estimate=pl.CostEstimate(
            flops=4 * heads * peers * block_len * lanes * HD,
            bytes_accessed=8 << 20,
            transcendentals=heads * peers * block_len * lanes,
        ),
        name="whole",
    )(block_order, lengths, row_positions, kv_store, queries, fresh_rows)


def solution(mesh):
    in_specs = (
        P(("groups", "shard"), None, None),
        P(("groups", "shard")),
        P("groups"),
        P("groups", None),
        P("groups", "shard"),
        P("groups", "shard"),
    )
    out_specs = P("groups", "shard")
    return jax.shard_map(shards, mesh=mesh, in_specs=in_specs, out_specs=out_specs, check_vma=False)
```

```python
import functools
import math

import jax
import jax.numpy as jnp
from jax import lax
from jax.experimental import pallas as pl
from jax.experimental.pallas import tpu as pltpu
from jax.sharding import PartitionSpec as P

QH = 64
KVH = 8
HD = 128
REQS = 8
GROUP = QH // KVH
PAIRS = REQS // 2

ROPE_BASE = 500000.0
NEG_FILL = -1e30
NEG_START = -1e29
LOG2E = 1.4426950408889634
NT = (((1,), (1,)), ((), ()))
TN = (((0,), (0,)), ((), ()))


def frequency_lanes():
    lane = lax.rem(lax.broadcasted_iota(jnp.int32, (1, HD), 1), HD // 2)
    return jnp.exp(-math.log(ROPE_BASE) * lane.astype(jnp.float32) / (HD // 2))


def turn_tables(positions):
    angle = positions.astype(jnp.float32) * frequency_lanes()
    lower = lax.broadcasted_iota(jnp.int32, angle.shape, 1) < HD // 2
    sine = jnp.sin(angle)
    return jnp.cos(angle), jnp.where(lower, -sine, sine)


def turned(x, cosine, sine):
    x = x.astype(jnp.float32)
    return (x * cosine + pltpu.roll(x, HD // 2, 1) * sine).astype(jnp.bfloat16)


def whole_kernel(
    n,
    scale,
    order_ref,
    lengths_ref,
    positions_ref,
    kv_hbm,
    q_hbm,
    fresh_hbm,
    out_ref,
    kv_ref,
    q_ref,
    fresh_ref,
    sel_ref,
    bcos_ref,
    bsin_ref,
    meta_ref,
    cos_ref,
    sin_ref,
    sent,
    received,
    metas,
    partner_q,
    qs,
    top,
    total,
    acc,
    o0,
    lse0,
    o1,
    lse1,
    o1_in,
    lse1_in,
    kv_send,
    kv_recv,
    meta_send,
    meta_recv,
    q_send,
    q_recv,
    o_send,
    o_recv,
    l_send,
    l_recv,
    local_sem,
    load_sem,
):
    heads, peers, block_len, _ = sent.shape
    rows = q_ref.shape[0]
    lanes = rows * GROUP
    q_width = GROUP * HD
    per_req = n // REQS
    device = lax.axis_index("shard")
    me = lax.rem(device, peers)
    first_peer = device - me
    partner = lax.rem(device + peers, n)
    log_scale = scale * LOG2E

    def remote(src, dst, send, recv, target):
        return pltpu.make_async_remote_copy(
            src_ref=src,
            dst_ref=dst,
            send_sem=send,
            recv_sem=recv,
            device_id={"shard": target},
            device_id_type=pl.DeviceIdType.MESH,
        )

    def kv_copy(c, i, slot):
        return remote(sent.at[c, i], received.at[c, slot], kv_send.at[c, i], kv_recv.at[c, slot], first_peer + i)

    def meta_copy(i, slot):
        return remote(
            meta_ref.at[i // per_req], metas.at[slot], meta_send.at[i], meta_recv.at[slot], first_peer + i
        )

    def q_copy(c):
        columns = pl.ds(pl.multiple_of(c * q_width, q_width), q_width)
        return remote(q_hbm.at[:, columns], partner_q.at[c], q_send.at[c], q_recv.at[c], partner)

    def o_copy(c):
        return remote(o1.at[c], o1_in.at[c], o_send.at[c], o_recv.at[c], partner)

    def l_copy(c):
        return remote(lse1.at[c], lse1_in.at[c], l_send.at[c], l_recv.at[c], partner)

    def own_kv(c):
        return pltpu.make_async_copy(sent.at[c, me], received.at[c, me], local_sem.at[c])

    loads = [
        pltpu.make_async_copy(hbm, here, load_sem.at[i])
        for i, (hbm, here) in enumerate(((kv_hbm, kv_ref), (q_hbm, q_ref), (fresh_hbm, fresh_ref)))
    ]
    for load in loads:
        load.start()

    barrier = pltpu.get_barrier_semaphore()
    pl.semaphore_signal(barrier, inc=1, device_id={"shard": partner}, device_id_type=pl.DeviceIdType.MESH)

    def greet(t, carry):
        pl.semaphore_signal(
            barrier,
            inc=1,
            device_id={"shard": first_peer + lax.rem(me + t, peers)},
            device_id_type=pl.DeviceIdType.MESH,
        )
        return carry

    lax.fori_loop(1, peers, greet, 0)
    pl.semaphore_wait(barrier, peers)

    def ask(c, carry):
        q_copy(c).start()
        return carry

    lax.fori_loop(0, min(2, heads), ask, 0)
    my_req = device // per_req
    other_req = lax.rem(my_req + PAIRS, REQS)
    reqs, offsets = [], []
    for b in range(order_ref.shape[0]):
        block = order_ref[b]
        start, req, own_start = jnp.int32(0), jnp.int32(-1), jnp.int32(0)
        for r in range(REQS):
            inside = block >= start
            req = jnp.where(inside, r, req)
            own_start = jnp.where(inside, start, own_start)
            start = start + lengths_ref[r]
        offset = (block - own_start) * block_len
        reqs.append(req)
        offsets.append(offset)
        cosine, sine = turn_tables(jnp.full((1, HD), offset, jnp.int32))
        bcos_ref[b] = cosine
        bsin_ref[b] = sine
    row_of_8 = lax.broadcasted_iota(jnp.int32, (8, HD), 0)
    for p in range(PAIRS):
        sel, pair_req, pair_offset = jnp.int32(0), jnp.int32(-1), jnp.int32(0)
        for b, (req, offset) in enumerate(zip(reqs, offsets)):
            match = lax.rem(req, PAIRS) == p
            sel = jnp.where(match, b, sel)
            pair_req = jnp.where(match, req, pair_req)
            pair_offset = jnp.where(match, offset, pair_offset)
        sel_ref[p] = sel
        meta_ref[p] = jnp.where(row_of_8 == 0, pair_req, pair_offset)

    loads[0].wait()

    own_meta = pltpu.make_async_copy(meta_ref.at[me // per_req], metas.at[me], local_sem.at[heads])
    own_meta.start()

    def tell(t, carry):
        meta_copy(lax.rem(me + t, peers), me).start()
        return carry

    lax.fori_loop(1, peers, tell, 0)

    def pack_chunk(c, carry):
        def pack(t, carry):
            i = lax.rem(me + t, peers)
            pair, group = i // per_req, lax.rem(i, per_req)
            sel = sel_ref[pair]
            column = pl.multiple_of((group * heads + c) * 2 * HD, 2 * HD)
            key = kv_ref[sel, :, pl.ds(column, HD)]
            sent[c, i, :, pl.ds(0, HD)] = turned(key, bcos_ref[sel], bsin_ref[sel])
            sent[c, i, :, pl.ds(HD, HD)] = kv_ref[sel, :, pl.ds(pl.multiple_of(column + HD, HD), HD)]

            @pl.when(t > 0)
            def _():
                kv_copy(c, i, me).start()

            @pl.when(t == 0)
            def _():
                own_kv(c).start()

            return carry

        return lax.fori_loop(0, peers, pack, carry)

    lax.fori_loop(0, heads, pack_chunk, 0)

    def hear(t, carry):
        j = lax.rem(me + t, peers)
        meta_copy(j, j).wait_recv()
        return carry

    limits = []
    for side, req in enumerate((my_req, other_req)):
        positions = positions_ref[pl.ds(req, 1), :]
        limits.append(jnp.concatenate([positions] * GROUP, axis=1))
        column = jnp.broadcast_to(positions.astype(jnp.float32), (HD, rows)).T
        cosine, sine = turn_tables(column)
        cos_ref[side] = cosine
        sin_ref[side] = sine
    loads[1].wait()
    loads[2].wait()
    own_meta.wait()
    lax.fori_loop(1, peers, hear, 0)

    def attend_chunk(c, carry):
        q_copy(c).wait_recv()

        @pl.when(c + 2 < heads)
        def _():
            q_copy(c + 2).start()

        f_column = pl.multiple_of(c * 2 * HD, 2 * HD)
        for g in range(GROUP):
            own_rows = pl.ds(g * rows, rows)
            column = pl.multiple_of(c * q_width + g * HD, HD)
            qs[0, own_rows, :] = turned(q_ref[:, pl.ds(column, HD)], cos_ref[0], sin_ref[0])
            qs[1, own_rows, :] = turned(partner_q[c, :, pl.ds(g * HD, HD)], cos_ref[1], sin_ref[1])
        own_key = turned(fresh_ref[:, pl.ds(f_column, HD)], cos_ref[0], sin_ref[0])
        own = lax.dot_general(own_key, qs[0], NT, preferred_element_type=jnp.float32)
        row_of = lax.broadcasted_iota(jnp.int32, (rows, lanes), 0)
        lane_of = lax.broadcasted_iota(jnp.int32, (rows, lanes), 1) % rows
        top[0] = jnp.sum(jnp.where(row_of == lane_of, own, 0.0), axis=0, keepdims=True)
        total[0] = jnp.ones((1, lanes), jnp.float32)
        own_value = fresh_ref[:, pl.ds(pl.multiple_of(f_column + HD, HD), HD)].astype(jnp.float32).T
        for g in range(GROUP):
            acc[0, :, pl.ds(g * rows, rows)] = own_value
        top[1] = jnp.full((1, lanes), NEG_START, jnp.float32)
        total[1] = jnp.zeros((1, lanes), jnp.float32)
        acc[1] = jnp.zeros((HD, lanes), jnp.float32)

        def attend(t, carry):
            j = lax.rem(me + peers - t, peers)

            @pl.when(t > 0)
            def _():
                kv_copy(c, j, j).wait_recv()

            @pl.when(t == 0)
            def _():
                own_kv(c).wait()

            req = metas[j, 0:1, :]
            offset = metas[j, 1:2, :]
            is_own = req == my_req
            is_partner = req == other_req
            pick0 = jnp.where(is_own, 1.0, 0.0).astype(jnp.bfloat16)
            pick1 = jnp.where(is_own, 0.0, 1.0).astype(jnp.bfloat16)
            query = qs[0] * pick0 + qs[1] * pick1
            wide_own = jnp.concatenate([is_own.astype(jnp.int32)] * GROUP, axis=1) > 0
            wide_partner = jnp.concatenate([is_partner.astype(jnp.int32)] * GROUP, axis=1) > 0
            wide_offset = jnp.concatenate([offset] * GROUP, axis=1)
            limit = jnp.where(wide_own, limits[0], limits[1]) - wide_offset
            keys = received[c, j, :, pl.ds(0, HD)]
            values = received[c, j, :, pl.ds(HD, HD)]
            scores = lax.dot_general(keys, query, NT, preferred_element_type=jnp.float32)
            token = lax.broadcasted_iota(jnp.int32, scores.shape, 0)
            scores = jnp.where(token < limit, scores, NEG_FILL)
            block_top = jnp.max(scores, axis=0, keepdims=True)
            weights = jnp.exp2((scores - block_top) * log_scale).astype(jnp.bfloat16)
            block_sum = jnp.sum(weights.astype(jnp.float32), axis=0, keepdims=True)
            block_out = lax.dot_general(values, weights, TN, preferred_element_type=jnp.float32)
            for side, chosen in enumerate((wide_own, wide_partner)):
                old_top = top[side]
                new_top = jnp.where(chosen, jnp.maximum(old_top, block_top), old_top)
                old_factor = jnp.exp2((old_top - new_top) * log_scale)
                new_factor = jnp.where(
                    chosen, jnp.exp2(jnp.where(chosen, block_top - new_top, 0.0) * log_scale), 0.0
                )
                top[side] = new_top
                total[side] = total[side] * old_factor + block_sum * new_factor
                acc[side] = acc[side] * old_factor + block_out * new_factor
            return carry

        lax.fori_loop(0, peers, attend, 0)
        o0[c] = acc[0] * (1.0 / total[0])
        lse0[c] = top[0] * scale + jnp.log(total[0])
        some = total[1] > 0.0
        safe = jnp.where(some, total[1], 1.0)
        o1[c] = (acc[1] * (1.0 / safe)).astype(jnp.bfloat16)
        sent_lse = jnp.where(some, top[1] * scale + jnp.log(safe), NEG_FILL)
        for g in range(GROUP):
            lse1[c, g : g + 1, :] = sent_lse[:, g * rows : (g + 1) * rows]
        l_copy(c).start()
        o_copy(c).start()
        return carry

    lax.fori_loop(0, heads, attend_chunk, 0)

    def merge_chunk(c, carry):
        l_copy(c).wait_recv()
        o_copy(c).wait_recv()
        base = lse0[c]
        other = jnp.concatenate([lse1_in[c, g : g + 1, :] for g in range(GROUP)], axis=1)
        larger = jnp.maximum(base, other)
        first, second = jnp.exp(base - larger), jnp.exp(other - larger)
        scaled = 1.0 / (first + second)
        joined = o0[c] * (first * scaled) + o1_in[c].astype(jnp.float32) * (second * scaled)
        for g in range(GROUP):
            column = pl.multiple_of(c * q_width + g * HD, HD)
            out_ref[:, pl.ds(column, HD)] = joined[:, g * rows : (g + 1) * rows].T.astype(out_ref.dtype)
        return carry

    lax.fori_loop(0, heads, merge_chunk, 0)

    def finish(c, carry):
        def sent_kv(t, carry):
            kv_copy(c, lax.rem(me + t, peers), me).wait_send()
            return carry

        lax.fori_loop(1, peers, sent_kv, 0)
        q_copy(c).wait_send()
        o_copy(c).wait_send()
        l_copy(c).wait_send()
        return carry

    lax.fori_loop(0, heads, finish, 0)

    def told(t, carry):
        meta_copy(lax.rem(me + t, peers), me).wait_send()
        return carry

    lax.fori_loop(1, peers, told, 0)


def shards(kv_store, block_order, lengths, row_positions, queries, fresh_rows):
    n_shard = lax.axis_size("shard")
    peers = n_shard // 2
    per_req = n_shard // REQS
    blk_dev, block_len, width = kv_store.shape
    heads = width // (per_req * 2 * HD)
    rows = queries.shape[0]
    lanes = rows * GROUP
    vmem = pl.BlockSpec(memory_space=pltpu.VMEM)
    smem = pl.BlockSpec(memory_space=pltpu.SMEM)
    anywhere = pl.BlockSpec(memory_space=pl.ANY)
    dma = pltpu.SemaphoreType.DMA
    return pl.pallas_call(
        functools.partial(whole_kernel, n_shard, 1.0 / math.sqrt(HD)),
        out_shape=jax.ShapeDtypeStruct(queries.shape, jnp.bfloat16),
        in_specs=[smem, smem, vmem, anywhere, anywhere, anywhere],
        out_specs=vmem,
        scratch_shapes=[
            pltpu.VMEM(kv_store.shape, kv_store.dtype),
            pltpu.VMEM(queries.shape, queries.dtype),
            pltpu.VMEM(fresh_rows.shape, fresh_rows.dtype),
            pltpu.SMEM((PAIRS,), jnp.int32),
            pltpu.VMEM((blk_dev, 1, HD), jnp.float32),
            pltpu.VMEM((blk_dev, 1, HD), jnp.float32),
            pltpu.VMEM((PAIRS, 8, HD), jnp.int32),
            pltpu.VMEM((2, rows, HD), jnp.float32),
            pltpu.VMEM((2, rows, HD), jnp.float32),
            pltpu.VMEM((heads, peers, block_len, 2 * HD), jnp.bfloat16),
            pltpu.VMEM((heads, peers, block_len, 2 * HD), jnp.bfloat16),
            pltpu.VMEM((peers, 8, HD), jnp.int32),
            pltpu.VMEM((heads, rows, GROUP * HD), jnp.bfloat16),
            pltpu.VMEM((2, lanes, HD), jnp.bfloat16),
            pltpu.VMEM((2, 1, lanes), jnp.float32),
            pltpu.VMEM((2, 1, lanes), jnp.float32),
            pltpu.VMEM((2, HD, lanes), jnp.float32),
            pltpu.VMEM((heads, HD, lanes), jnp.float32),
            pltpu.VMEM((heads, 1, lanes), jnp.float32),
            pltpu.VMEM((heads, HD, lanes), jnp.bfloat16),
            pltpu.VMEM((heads, GROUP, rows), jnp.float32),
            pltpu.VMEM((heads, HD, lanes), jnp.bfloat16),
            pltpu.VMEM((heads, GROUP, rows), jnp.float32),
            dma((heads, peers)),
            dma((heads, peers)),
            dma((peers,)),
            dma((peers,)),
            dma((heads,)),
            dma((heads,)),
            dma((heads,)),
            dma((heads,)),
            dma((heads,)),
            dma((heads,)),
            dma((heads + 1,)),
            dma((3,)),
        ],
        compiler_params=pltpu.CompilerParams(
            collective_id=0, has_side_effects=True, vmem_limit_bytes=60 << 20
        ),
        cost_estimate=pl.CostEstimate(
            flops=4 * heads * peers * block_len * lanes * HD,
            bytes_accessed=8 << 20,
            transcendentals=heads * peers * block_len * lanes,
        ),
        name="whole",
    )(block_order, lengths, row_positions, kv_store, queries, fresh_rows)


def solution(mesh):
    in_specs = (
        P(("groups", "shard"), None, None),
        P(("groups", "shard")),
        P("groups"),
        P("groups", None),
        P("groups", "shard"),
        P("groups", "shard"),
    )
    out_specs = P("groups", "shard")
    return jax.shard_map(shards, mesh=mesh, in_specs=in_specs, out_specs=out_specs, check_vma=False)
```
